32 devices in a mesh: grp: 2 (over y), re: 16 (over z, x, core).
Axes of the slice: x: 2, y: 2, z: 4, core: 2. Of those that a mesh axis runs over, the one named last changes fastest.
Arguments:
- epmat: bfloat16 [2, 16, 8, 122880], P(None, 're'), may hold values from -0.5 to 0.5
- re_coords: int32 [16, 3], replicated, may hold values from 0 to 15
- rp_coords: int32 [8, 3], replicated, may hold values from 0 to 15
- q_coords: int32 [8, 3], P('grp'), parts along dimension 0, may hold values from 0 to 15
- u_k: bfloat16 [32, 2, 32, 32], P('re'), may hold values from -0.75 to 0.75
- u_kq: bfloat16 [32, 8, 2, 32, 32], P('re', 'grp'), parts along dimension 1, may hold values from -0.75 to 0.75
- evec: bfloat16 [8, 2, 120, 120], P('grp'), parts along dimension 0, may hold values from -0.375 to 0.375
- omega: float32 [8, 120], P('grp'), parts along dimension 0, may hold values from 0.01 to 0.1
- eps_k: float32 [32, 32], replicated, may hold values from -0.3 to 0.3
- eps_kq: float32 [32, 8, 32], P(None, 'grp'), parts along dimension 1, may hold values from -0.3 to 0.3
- temps: float32 [8], replicated, may hold values from 0.005 to 0.05
- owner_states: int32 [32, 16], P('grp'), parts along dimension 0, may hold values from 0 to 4095, as said below
Outputs:
- coupling_sq: bfloat16 [32, 8, 32, 3840], P('re', 'grp'), parts along dimension 1
- rates: float32 [16, 256], P('grp', 're'), parts along dimension 0
The draws below stay inside these ranges and needn't reach their ends.
There are 2 independent parts, one for each index of `grp`. The reference program is written for one: setup_inputs(seed, part) draws one part's arguments, and reference() takes and returns one part's arrays. A program takes and returns all parts, laid end to end along the dimension named above; an argument that names none is the same for every part. Nothing has to cross between parts.
Inputs may be any that keep to these rules, and one draw needn't show every extreme that they name: `owner_states`: row o lists the 16 window states whose terms index o of re owns; state (k-point j, q-point q, band b) has the number (j * 4 + q) * 32 + b and lies on index j // 2. No state appears twice in the array. A row is 8 runs of 2 entries; the states of one run lie on one index, the runs of a row on distinct indices. A quarter of the indices hold a run of every row.
All inputs are finite; a program needn't handle non-finite values.
Results may differ from the reference program's by a relative error of at most 0.0091.
Values may be sent and summed in bfloat16 or wider, within the bound.
A program may use at most 192 MiB of HBM per device.

```python
import math
from functools import partial
import jax
import jax.numpy as jnp
from jax import lax

NW = 32
NM = 120
GRID = 16
Q = 4
RP = 8
NTEMP = 8
SLOT = 2
RE_DEV = 1
KDEV = 2
RE = 16
K = 32
FLAT = 122880
CAP = 16
N_RE = 16


def shuffled(sub_key, length):
    return jax.random.permutation(sub_key, length)


def draw_owner_states(key, part):
    key = jax.random.fold_in(key, 7)
    node_count = 2 * CAP // SLOT
    hot_count = node_count // 4
    cold_count = node_count - hot_count
    block_count = CAP // SLOT
    state_count = KDEV * Q * NW
    key_dev, key_order, key_state = jax.random.split(key, 3)
    dev_order = jax.random.permutation(key_dev, node_count)
    owners = jnp.arange(node_count, dtype=jnp.int32)[:, None]
    block_slots = jnp.arange(block_count, dtype=jnp.int32)[None, :]
    hot_pick = dev_order[(owners + block_slots) % hot_count]
    cold_pick = dev_order[hot_count + (owners + block_slots - hot_count) % cold_count]
    source = jnp.where(block_slots < hot_count, hot_pick, cold_pick)
    row_keys = jax.random.split(key_order, node_count)
    shuffles = jax.vmap(partial(shuffled, length=block_count))(row_keys)
    source = jnp.take_along_axis(source, shuffles, axis=1)
    flat_src = source.reshape(-1)
    onehot = (flat_src[:, None] == jnp.arange(node_count, dtype=jnp.int32)[None, :]).astype(jnp.int32)
    before = jnp.cumsum(onehot, axis=0) - onehot
    block_rank = jnp.sum(before * onehot, axis=1)
    state_keys = jax.random.split(key_state, node_count)
    orders = jax.vmap(partial(shuffled, length=state_count))(state_keys)
    within = jnp.arange(SLOT, dtype=jnp.int32)[None, :]
    local_state = orders[flat_src[:, None], block_rank[:, None] * SLOT + within]
    states = flat_src[:, None] * state_count + local_state
    return states.reshape(node_count, CAP).astype(jnp.int32)


def set_ends(array, rng, least, high):
    longest = array.shape.index(max(array.shape))
    spots = []
    for shift in (0, 1):
        where = [jax.random.randint(jax.random.fold_in(rng, axis), (), 0, length) for axis, length in enumerate(array.shape)]
        where[longest] = (where[longest] + shift) % array.shape[longest]
        spots.append(tuple(where))
    return array.at[spots[0]].set(least).at[spots[1]].set(high)


def block_levels(key, dims, pieces, smallest, largest):
    level = 1.0
    for dim, blocks in pieces:
        heights = jax.random.uniform(jax.random.fold_in(jax.random.fold_in(key, 6), dim), (blocks,), jnp.float32, smallest / len(pieces), largest / len(pieces))
        level = level * jnp.repeat(jnp.exp(heights), dims[dim] // blocks).reshape((-1,) + (1,) * (len(dims) - 1 - dim))
    return level


def scatter_about(own_key, extent, scale, reach, cuts=(), kind=jnp.bfloat16):
    factor_of = block_levels(own_key, extent, cuts, -0.22, 0.18) if cuts else 1.0
    values = jax.random.normal(own_key, extent, jnp.float32) * scale * factor_of
    return jnp.minimum(jnp.maximum(values, -reach), reach).astype(kind)


def setup_inputs(seed: int = 0, part: int = 0) -> dict:
    arg_keys = jax.random.split(jax.random.key(seed), 13)
    part_splits = jax.random.split(jax.random.fold_in(arg_keys[12], part), 13)
    return {
        "epmat": scatter_about(arg_keys[0], (2, RE, RP, FLAT), (RE * RP) ** -0.5, 0.5, ((1, 16),)),
        "re_coords": set_ends(jax.random.randint(arg_keys[1], (RE, 3), 0, GRID), jax.random.fold_in(arg_keys[1], 1), 0, GRID - 1).astype(jnp.int32),
        "rp_coords": set_ends(jax.random.randint(arg_keys[2], (RP, 3), 0, GRID), jax.random.fold_in(arg_keys[2], 1), 0, GRID - 1).astype(jnp.int32),
        "q_coords": set_ends(jax.random.randint(part_splits[3], (Q, 3), 0, GRID), jax.random.fold_in(part_splits[3], 1), 0, GRID - 1).astype(jnp.int32),
        "u_k": scatter_about(arg_keys[4], (K, 2, NW, NW), (2 * NW) ** -0.5, 0.75, ((0, 16),)),
        "u_kq": scatter_about(part_splits[5], (K, Q, 2, NW, NW), (2 * NW) ** -0.5, 0.75, ((0, 16),)),
        "evec": scatter_about(part_splits[6], (Q, 2, NM, NM), (2 * NM) ** -0.5, 0.375),
        "omega": jnp.clip(jnp.exp(jax.random.uniform(part_splits[7], (Q, NM), jnp.float32, math.log(0.01), math.log(0.1))), 0.01, 0.1),
        "eps_k": jnp.clip(jax.random.uniform(arg_keys[8], (K, NW), jnp.float32, -0.3, 0.3), -0.3, 0.3),
        "eps_kq": jnp.clip(jax.random.uniform(part_splits[9], (K, Q, NW), jnp.float32, -0.3, 0.3), -0.3, 0.3),
        "temps": jnp.clip(jnp.exp(jax.random.uniform(arg_keys[10], (NTEMP,), jnp.float32, math.log(0.005), math.log(0.05))), 0.005, 0.05),
        "owner_states": draw_owner_states(jax.random.fold_in(jax.random.fold_in(arg_keys[12], part), 71), part),
    }


broadening = 0.02


def phase_pair(left_vecs, right_vecs):
    dot_mod = jnp.sum(left_vecs[:, None, :] * right_vecs[None, :, :], axis=2) % GRID
    angles = (2.0 * jnp.pi / GRID) * dot_mod.astype(jnp.float32)
    return jnp.cos(angles).astype(jnp.bfloat16), jnp.sin(angles).astype(jnp.bfloat16)


def fine_points(point_count):
    point_index = jnp.arange(point_count, dtype=jnp.int32)
    return jnp.stack([point_index % GRID, (point_index // GRID) % GRID, point_index // (GRID * GRID)], axis=1)


def pair_rows(first_part, second_part, stack_axis):
    upper = jnp.stack([first_part, second_part], axis=stack_axis)
    lower = jnp.stack([-second_part, first_part], axis=stack_axis)
    return jnp.stack([upper, lower], axis=stack_axis)


def settle(values):
    return lax.optimization_barrier(values.astype(jnp.bfloat16)).astype(jnp.float32)


def couple(blocks, rot_k, rot_kq, modes):
    highest = lax.Precision.HIGHEST
    right_mix = pair_rows(rot_k[:, 0], rot_k[:, 1], 1).astype(jnp.float32)
    half_rot = settle(jnp.einsum('dkqvab,kdcbe->ckqvae', blocks, right_mix, precision=highest))
    left_mix = pair_rows(rot_kq[:, :, 0], rot_kq[:, :, 1], 2).astype(jnp.float32)
    turned = settle(jnp.einsum('dkqvxe,kqcdxa->ckqvae', half_rot, left_mix, precision=highest))
    mode_mix = pair_rows(modes[:, 0], -modes[:, 1], 1).astype(jnp.float32)
    projected = jnp.einsum('dkqvae,qcdvm->ckqema', turned, mode_mix, precision=highest)
    strength = projected[0] * projected[0] + projected[1] * projected[1]
    return strength.astype(jnp.bfloat16).reshape(blocks.shape[1], blocks.shape[2], blocks.shape[5], -1)


def rate_block(coupling_block, state_ids, eps_k, eps_kq, omega, temps):
    q_count = omega.shape[0]
    band_count = eps_k.shape[1]
    k_index = state_ids // (q_count * band_count)
    q_index = (state_ids // band_count) % q_count
    n_index = state_ids % band_count
    energy_n = eps_k[k_index, n_index]
    energy_m = eps_kq[k_index, q_index]
    phonon_freq = omega[q_index]
    strength = coupling_block.astype(jnp.float32)
    energy_gap = energy_n[:, None, None] - energy_m[:, None, :]
    peak_scale = broadening / jnp.pi
    lorentz_abs = peak_scale / ((energy_gap + phonon_freq[:, :, None]) ** 2 + broadening ** 2)
    lorentz_emit = peak_scale / ((energy_gap - phonon_freq[:, :, None]) ** 2 + broadening ** 2)
    along_mode = jnp.sum(strength * (lorentz_abs + lorentz_emit), axis=2)
    along_band = jnp.sum(strength * (lorentz_abs - lorentz_emit), axis=1)
    base_term = jnp.sum(strength * lorentz_emit, axis=(1, 2))
    bose_occ = 1.0 / jnp.expm1(phonon_freq[None, :, :] / temps[:, None, None])
    fermi_occ = jax.nn.sigmoid(-energy_m[None, :, :] / temps[:, None, None])
    rate_sum = jnp.sum(bose_occ * along_mode[None], axis=2) + base_term[None] + jnp.sum(fermi_occ * along_band[None], axis=2)
    return rate_sum / (strength.shape[1] * strength.shape[2])


def reference(epmat, re_coords, rp_coords, q_coords, u_k, u_kq, evec, omega, eps_k, eps_kq, temps, owner_states):
    cos_q, sin_q = phase_pair(q_coords, rp_coords)
    phase_mix = pair_rows(cos_q, -sin_q, 0).astype(jnp.float32)

    def shard_planes(shard_index):
        start = (shard_index * RE_DEV).astype(jnp.int32)
        shard = lax.dynamic_slice_in_dim(epmat, start, RE_DEV, 1).astype(jnp.float32)
        summed = jnp.einsum('cdqp,drpf->crqf', phase_mix, shard, precision=lax.Precision.HIGHEST)
        return summed.astype(jnp.bfloat16)

    planes = lax.map(shard_planes, jnp.arange(N_RE, dtype=jnp.int32))
    planes = planes.transpose(1, 0, 2, 3, 4).reshape(2 * RE, Q * FLAT)
    flat_planes = lax.optimization_barrier(planes).astype(jnp.float32)
    cos_k, sin_k = phase_pair(fine_points(K), re_coords)
    phase_table = pair_rows(cos_k, -sin_k, 0).transpose(0, 2, 1, 3).reshape(2, N_RE, KDEV, 2 * RE).transpose(1, 0, 2, 3)

    def one_group(inputs):
        group_rows, group_k, group_kq = inputs
        spread = jnp.dot(group_rows.reshape(2 * KDEV, 2 * RE).astype(jnp.float32), flat_planes, precision=lax.Precision.HIGHEST)
        spread = settle(spread).reshape(2, KDEV, Q, NW, NM, NW).transpose(0, 1, 2, 4, 5, 3)
        return couple(spread, group_k, group_kq, evec)

    coupling = lax.map(one_group, (phase_table, u_k.reshape(N_RE, KDEV, 2, NW, NW), u_kq.reshape(N_RE, KDEV, Q, 2, NW, NW)))
    coupling = coupling.reshape(K, Q, NW, NM * NW)
    state_rows = coupling.reshape(K * Q * NW, NM, NW)

    def owner_rates(own_ids):
        return rate_block(state_rows[own_ids], own_ids, eps_k, eps_kq, omega, temps)

    rates = lax.map(owner_rates, owner_states)
    rates = rates.transpose(1, 0, 2).reshape(NTEMP, N_RE * CAP)
    return coupling, rates
```

```python
import functools

import jax
import jax.numpy as jnp
from jax import lax
from jax.experimental import pallas as pl
from jax.experimental.pallas import tpu as pltpu
from jax.sharding import PartitionSpec as P

GRID = 16
SLOT = 2
LANES = 128


broadening = 0.02


def phase_pair(left_vecs, right_vecs):
    dot_mod = jnp.sum(left_vecs[:, None, :] * right_vecs[None, :, :], axis=2) % GRID
    angles = 2.0 * jnp.pi / GRID * dot_mod.astype(jnp.float32)
    return (jnp.cos(angles).astype(jnp.bfloat16), jnp.sin(angles).astype(jnp.bfloat16))


def fine_points(point_count):
    point_index = jnp.arange(point_count, dtype=jnp.int32)
    return jnp.stack(
        [point_index % GRID, point_index // GRID % GRID, point_index // (GRID * GRID)], axis=1
    )


def pair_rows(first_part, second_part, stack_axis):
    upper = jnp.stack([first_part, second_part], axis=stack_axis)
    lower = jnp.stack([-second_part, first_part], axis=stack_axis)
    return jnp.stack([upper, lower], axis=stack_axis)


def swap_matrix(bands):
    per = LANES // bands
    size = per * LANES
    row = lax.broadcasted_iota(jnp.int32, (size, size), 0)
    col = lax.broadcasted_iota(jnp.int32, (size, size), 1)
    image = (row // bands % per) * LANES + (row // LANES) * bands + row % bands
    return (image == col).astype(jnp.float32).astype(jnp.bfloat16)


def modes_first(x_ref, mix_ref, modes_ref, swap_ref, out_ref, tiles, turned):
    q_count = modes_ref.shape[0]
    bands = out_ref.shape[2] // 2
    per = LANES // bands
    wide = x_ref.shape[2] // bands
    n_tiles = wide // LANES
    pad_tiles = tiles.shape[1]
    groups = bands // per
    out_tiles = out_ref.shape[3] // LANES

    if pad_tiles > n_tiles:
        rest = (bands, pad_tiles - n_tiles, 2 * q_count, LANES)
        tiles[:, n_tiles:] = jnp.zeros(rest, jnp.float32)

    def sum_band(band, carry):
        lanes = pl.ds(pl.multiple_of(band * wide, LANES), wide)
        total = jnp.dot(mix_ref[0], x_ref[0, :, lanes], preferred_element_type=jnp.float32)
        total += jnp.dot(mix_ref[1], x_ref[1, :, lanes], preferred_element_type=jnp.float32)
        for tile in range(n_tiles):
            tiles[band, tile] = total[:, tile * LANES : (tile + 1) * LANES]
        return carry

    lax.fori_loop(0, bands, sum_band, 0)

    for q in range(q_count):
        rows = []
        for part in range(2):
            for group in range(groups):
                rows.append(
                    jnp.concatenate(
                        [
                            tiles[group * per + i, :, part * q_count + q, :].astype(jnp.bfloat16)
                            for i in range(per)
                        ],
                        axis=1,
                    )
                )
        swapped = jnp.dot(
            jnp.concatenate(rows, axis=0), swap_ref[...], preferred_element_type=jnp.float32
        ).astype(jnp.bfloat16)
        stacked = []
        for part in range(2):
            for i in range(per):
                stacked.append(
                    jnp.concatenate(
                        [
                            swapped[
                                (part * groups + group) * pad_tiles : (part * groups + group + 1)
                                * pad_tiles,
                                i * LANES : (i + 1) * LANES,
                            ]
                            for group in range(groups)
                        ],
                        axis=1,
                    )
                )
        moded = jnp.dot(
            modes_ref[q], jnp.concatenate(stacked, axis=0), preferred_element_type=jnp.float32
        ).astype(jnp.bfloat16)
        rows = []
        for part in range(2):
            for group in range(groups):
                rows.append(
                    jnp.concatenate(
                        [
                            moded[
                                (part * per + i) * pad_tiles : (part * per + i + 1) * pad_tiles,
                                group * LANES : (group + 1) * LANES,
                            ]
                            for i in range(per)
                        ],
                        axis=1,
                    )
                )
        back = jnp.dot(
            jnp.concatenate(rows, axis=0), swap_ref[...], preferred_element_type=jnp.float32
        )
        for part in range(2):
            for group in range(groups):
                for i in range(per):
                    turned[part * bands + group * per + i] = back[
                        (part * groups + group) * pad_tiles : (part * groups + group + 1)
                        * pad_tiles,
                        i * LANES : (i + 1) * LANES,
                    ]
        for tile in range(pad_tiles):
            place = tile % out_tiles
            out_ref[tile // out_tiles, q, :, place * LANES : (place + 1) * LANES] = turned[
                :, tile, :
            ].astype(jnp.bfloat16)


def rotate_square(batch, t_ref, cos_ref, sin_ref, one_ref, two_ref, real_ref, imag_ref, out_ref):
    bands = real_ref.shape[1]
    depth, lanes = t_ref.shape
    n_tiles = lanes // LANES
    per = LANES // bands
    row = lax.broadcasted_iota(jnp.int32, (LANES, LANES), 0) // bands
    col = lax.broadcasted_iota(jnp.int32, (LANES, LANES), 1) // bands
    same = row == col
    coeffs = []
    for k in range(batch):
        one = one_ref[k].astype(jnp.float32)
        two = two_ref[k].astype(jnp.float32)
        parts = []
        for tile in range(depth // LANES):
            lane = slice(tile * LANES, (tile + 1) * LANES)
            parts.append((cos_ref[k, :, lane] * one + sin_ref[k, :, lane] * two).astype(jnp.bfloat16))
        coeffs.append(jnp.concatenate(parts, axis=1))
    half = jnp.dot(
        jnp.concatenate(coeffs, axis=0), t_ref[...], preferred_element_type=jnp.float32
    ).astype(jnp.bfloat16)
    for k in range(batch):
        real = jnp.concatenate([real_ref[k].astype(jnp.float32)] * per, axis=0)
        imag = jnp.concatenate([imag_ref[k].astype(jnp.float32)] * per, axis=0)
        real = jnp.where(same, real, 0.0)
        imag = jnp.where(same, imag, 0.0)
        left = jnp.concatenate([real, imag], axis=0)
        right = jnp.concatenate([-imag, real], axis=0)
        both = jnp.concatenate([left, right], axis=1).astype(jnp.bfloat16)
        rows = []
        top = 2 * bands * k
        for tile in range(n_tiles):
            lane = slice(tile * LANES, (tile + 1) * LANES)
            rows.append(
                jnp.concatenate(
                    [half[top : top + bands, lane], half[top + bands : top + 2 * bands, lane]], axis=1
                )
            )
        final = jnp.dot(jnp.concatenate(rows, axis=0), both, preferred_element_type=jnp.float32)
        power = final[:, :LANES] * final[:, :LANES] + final[:, LANES:] * final[:, LANES:]
        power = power.astype(jnp.bfloat16)
        for tile in range(n_tiles):
            out_ref[k, :, tile * LANES : (tile + 1) * LANES] = power[tile * bands : (tile + 1) * bands]


def rate_block(coupling_block, state_ids, eps_k, eps_kq, omega, temps):
    q_count = omega.shape[0]
    band_count = eps_k.shape[1]
    k_index = state_ids // (q_count * band_count)
    q_index = state_ids // band_count % q_count
    n_index = state_ids % band_count
    energy_n = eps_k[k_index, n_index]
    energy_m = eps_kq[k_index, q_index]
    phonon_freq = omega[q_index]
    strength = coupling_block.astype(jnp.float32)
    energy_gap = energy_n[:, None, None] - energy_m[:, None, :]
    peak_scale = broadening / jnp.pi
    lorentz_abs = peak_scale / ((energy_gap + phonon_freq[:, :, None]) ** 2 + broadening**2)
    lorentz_emit = peak_scale / ((energy_gap - phonon_freq[:, :, None]) ** 2 + broadening**2)
    along_mode = jnp.sum(strength * (lorentz_abs + lorentz_emit), axis=2)
    along_band = jnp.sum(strength * (lorentz_abs - lorentz_emit), axis=1)
    base_term = jnp.sum(strength * lorentz_emit, axis=(1, 2))
    bose_occ = 1.0 / jnp.expm1(phonon_freq[None, :, :] / temps[:, None, None])
    fermi_occ = jax.nn.sigmoid(-energy_m[None, :, :] / temps[:, None, None])
    rate_sum = (
        jnp.sum(bose_occ * along_mode[None], axis=2)
        + base_term[None]
        + jnp.sum(fermi_occ * along_band[None], axis=2)
    )
    return rate_sum / (strength.shape[1] * strength.shape[2])


def local(
    epmat,
    re_coords,
    rp_coords,
    q_coords,
    u_k,
    u_kq,
    evec,
    omega,
    eps_k,
    eps_kq,
    temps,
    owner_states,
):
    node_count = lax.axis_size("re")
    self_index = lax.axis_index("re")
    q_count = q_coords.shape[0]
    local_re = epmat.shape[1]
    local_k = u_k.shape[0]
    count_k = local_k * node_count
    bands = u_k.shape[2]
    modes = evec.shape[2]
    wide = modes * bands
    per = LANES // bands
    n_tiles = wide // LANES
    splits = node_count // q_count
    pad_tiles = max(-(-n_tiles // 8) * 8, splits)
    lanes = pad_tiles // splits * LANES
    bf16 = jnp.bfloat16

    cos_q, sin_q = phase_pair(q_coords, rp_coords)
    mix = jnp.stack(
        [jnp.concatenate([cos_q, sin_q], axis=0), jnp.concatenate([-sin_q, cos_q], axis=0)], axis=0
    )
    pad = pad_tiles * per - modes
    padded = jnp.pad(evec, ((0, 0), (0, 0), (0, pad), (0, pad)))
    padded = padded.reshape(q_count, 2, pad_tiles, per, pad_tiles, per)
    padded = padded.transpose(0, 1, 5, 4, 3, 2).reshape(
        q_count, 2, pad_tiles * per, pad_tiles * per
    )
    upper = jnp.concatenate([padded[:, 0], -padded[:, 1]], axis=2)
    lower = jnp.concatenate([padded[:, 1], padded[:, 0]], axis=2)
    mode_mix = jnp.concatenate([upper, lower], axis=1)

    both = jnp.concatenate([u_k[:, None], u_kq], axis=1)
    both = lax.all_gather(both, "re", axis=0, tiled=True)
    rot_k = both[:, 0].transpose(0, 1, 3, 2)
    rot_kq = lax.dynamic_index_in_dim(both, 1 + self_index % q_count, 1, keepdims=False)
    ur, ui = rot_k[:, 0], rot_k[:, 1]
    one = jnp.concatenate(
        [jnp.concatenate([ur, -ui], axis=2), jnp.concatenate([ui, ur], axis=2)], axis=1
    )
    two = jnp.concatenate(
        [jnp.concatenate([-ui, -ur], axis=2), jnp.concatenate([ur, -ui], axis=2)], axis=1
    )
    one = jnp.concatenate([one] * (LANES // (2 * bands)), axis=2)
    two = jnp.concatenate([two] * (LANES // (2 * bands)), axis=2)
    wide_kq = jnp.concatenate([rot_kq] * per, axis=3)
    cos_k, sin_k = phase_pair(fine_points(count_k), re_coords)
    cos_row = jnp.repeat(cos_k.astype(jnp.float32), 2 * bands, axis=1)[:, None, :]
    sin_row = jnp.repeat(sin_k.astype(jnp.float32), 2 * bands, axis=1)[:, None, :]

    call = pl.pallas_call(
        modes_first,
        out_shape=jax.ShapeDtypeStruct((splits, q_count, 2 * bands, lanes), bf16),
        scratch_shapes=[
            pltpu.VMEM((bands, pad_tiles, 2 * q_count, LANES), jnp.float32),
            pltpu.VMEM((2 * bands, pad_tiles, LANES), jnp.float32),
        ],
        compiler_params=pltpu.CompilerParams(vmem_limit_bytes=50 * 2**20),
        name="modes_first",
    )
    swap = swap_matrix(bands)
    sent = [call(epmat[:, r], mix, mode_mix, swap) for r in range(local_re)]
    sent = sent[0][:, :, None] if local_re == 1 else jnp.stack(sent, axis=2)
    sent = sent.reshape(node_count, local_re * 2 * bands, lanes)
    came = lax.all_to_all(sent, "re", split_axis=0, concat_axis=0, tiled=True)
    depth = node_count * local_re * 2 * bands
    came = came.reshape(depth, lanes)

    batch = 4
    power = pl.pallas_call(
        functools.partial(rotate_square, batch),
        grid=(count_k // batch,),
        in_specs=[
            pl.BlockSpec((depth, lanes), lambda i: (0, 0)),
            pl.BlockSpec((batch, 1, depth), lambda i: (i, 0, 0)),
            pl.BlockSpec((batch, 1, depth), lambda i: (i, 0, 0)),
            pl.BlockSpec((batch, 2 * bands, LANES), lambda i: (i, 0, 0)),
            pl.BlockSpec((batch, 2 * bands, LANES), lambda i: (i, 0, 0)),
            pl.BlockSpec((batch, bands, LANES), lambda i: (i, 0, 0)),
            pl.BlockSpec((batch, bands, LANES), lambda i: (i, 0, 0)),
        ],
        out_specs=pl.BlockSpec((batch, bands, lanes), lambda i: (i, 0, 0)),
        out_shape=jax.ShapeDtypeStruct((count_k, bands, lanes), bf16),
        compiler_params=pltpu.CompilerParams(vmem_limit_bytes=50 * 2**20),
        name="rotate_square",
    )(came, cos_row, sin_row, one, two, wide_kq[:, 0], wide_kq[:, 1])

    spread = lax.all_to_all(power, "re", split_axis=0, concat_axis=0, tiled=True)
    spread = spread.reshape(splits, q_count, local_k, bands, lanes)
    coupling = spread.transpose(2, 1, 3, 0, 4).reshape(local_k, q_count, bands, splits * lanes)
    coupling = coupling[..., :wide]

    state_rows = coupling.reshape(-1, wide)
    state_total = state_rows.shape[0]
    capacity = owner_states.shape[1]
    run_count = capacity // SLOT
    runs = owner_states.reshape(node_count, run_count, SLOT)
    holds = runs[:, :, 0] // state_total == self_index
    picked = jnp.sum(jnp.where(holds[:, :, None], runs - self_index * state_total, 0), axis=1)
    picked = picked.reshape(-1)
    strength = state_rows[picked].reshape(-1, modes, bands)
    here = rate_block(
        strength, picked + self_index * state_total, eps_k, eps_kq, omega, temps
    )
    here = here.T.reshape(node_count, 1, SLOT, temps.shape[0])
    placed = jnp.where(holds[:, :, None, None], here, 0.0)
    placed = placed.reshape(node_count, capacity * temps.shape[0])
    rates = lax.psum_scatter(placed, "re", scatter_dimension=0, tiled=True)
    rates = rates.reshape(capacity, temps.shape[0]).T
    return (coupling, rates)


def solution(mesh):
    in_specs = (
        P(None, "re", None, None),
        P(),
        P(),
        P("grp", None),
        P("re", None, None, None),
        P("re", "grp", None, None, None),
        P("grp", None, None, None),
        P("grp", None),
        P(),
        P(None, "grp", None),
        P(),
        P("grp", None),
    )
    out_specs = (P("re", "grp", None, None), P("grp", "re"))
    return jax.shard_map(local, mesh=mesh, in_specs=in_specs, out_specs=out_specs, check_vma=False)
```

```python
import functools

import jax
import jax.numpy as jnp
import numpy as np
from jax import lax
from jax.experimental import pallas as pl
from jax.experimental.pallas import tpu as pltpu
from jax.sharding import PartitionSpec as P

GRID = 16
SLOT = 2
LANES = 128


broadening = 0.02


def phase_pair(left_vecs, right_vecs):
    dot_mod = jnp.sum(left_vecs[:, None, :] * right_vecs[None, :, :], axis=2) % GRID
    angles = 2.0 * jnp.pi / GRID * dot_mod.astype(jnp.float32)
    return (jnp.cos(angles).astype(jnp.bfloat16), jnp.sin(angles).astype(jnp.bfloat16))


def fine_points(point_count):
    point_index = jnp.arange(point_count, dtype=jnp.int32)
    return jnp.stack(
        [point_index % GRID, point_index // GRID % GRID, point_index // (GRID * GRID)], axis=1
    )


def pair_rows(first_part, second_part, stack_axis):
    upper = jnp.stack([first_part, second_part], axis=stack_axis)
    lower = jnp.stack([-second_part, first_part], axis=stack_axis)
    return jnp.stack([upper, lower], axis=stack_axis)


MESH = pl.DeviceIdType.MESH


def swap_matrix(bands):
    per = LANES // bands
    row = np.arange(per * LANES)
    image = (row // bands % per) * LANES + (row // LANES) * bands + row % bands
    return jnp.asarray(np.eye(per * LANES)[image], jnp.bfloat16)


def mode_order(modes, per, pad_tiles):
    row = np.arange(per * pad_tiles)
    source = (row % pad_tiles) * per + row // pad_tiles
    return jnp.asarray(source[:, None] == np.arange(modes)[None, :], jnp.bfloat16)


def widen_matrix(bands):
    per = LANES // bands
    out = np.zeros((LANES, 5 * LANES))
    plans = [
        [(0, 1), (1, -1)] * (per // 2),
        [(1, 1), (0, 1)] * (per // 2),
        [(1, -1), (0, -1)] * (per // 2),
        [(2, 1)] * per,
        [(3, 1)] * per,
    ]
    for tile, plan in enumerate(plans):
        for place, (source, sign) in enumerate(plan):
            for band in range(bands):
                out[source * bands + band, tile * LANES + place * bands + band] = sign
    return jnp.asarray(out, jnp.bfloat16)


def exchange(
    node_count,
    local_k,
    batch,
    x_ref,
    mix_ref,
    evec_ref,
    packs_ref,
    cos_ref,
    sin_ref,
    swap_ref,
    order_ref,
    widen_ref,
    out_ref,
    tiles,
    turned,
    staged,
    gathered,
    packs,
    power,
    pack_send,
    pack_recv,
    mode_send,
    mode_recv,
    power_send,
    power_recv,
    own_sem,
):
    q_count = evec_ref.shape[0]
    bands = packs_ref.shape[2]
    per = LANES // bands
    wide = x_ref.shape[2] // bands
    n_tiles = wide // LANES
    pad_tiles = tiles.shape[1]
    groups = bands // per
    lanes = staged.shape[3]
    out_tiles = lanes // LANES
    splits = staged.shape[0]
    depth = node_count * 2 * bands

    me = lax.axis_index("re")
    my_q = lax.rem(me, q_count)
    my_split = me // q_count

    barrier = pltpu.get_barrier_semaphore()

    def greet(i, carry):
        other = lax.rem(me + i, node_count)
        pl.semaphore_signal(barrier, inc=1, device_id={"re": other}, device_id_type=MESH)
        return carry

    lax.fori_loop(1, node_count, greet, 0)
    pl.semaphore_wait(barrier, node_count - 1)

    def pack_copy(to):
        return pltpu.make_async_remote_copy(
            src_ref=packs_ref.at[lax.rem(to, q_count)],
            dst_ref=packs.at[me],
            send_sem=pack_send.at[to],
            recv_sem=pack_recv.at[me],
            device_id={"re": to},
            device_id_type=MESH,
        )

    def pack_from(source):
        return pltpu.make_async_remote_copy(
            src_ref=packs_ref.at[0],
            dst_ref=packs.at[source],
            send_sem=pack_send.at[source],
            recv_sem=pack_recv.at[source],
            device_id={"re": source},
            device_id_type=MESH,
        )

    def send_pack(i, carry):
        pack_copy(lax.rem(me + i, node_count)).start()
        return carry

    lax.fori_loop(1, node_count, send_pack, 0)
    packs[me] = packs_ref[my_q]

    if pad_tiles > n_tiles:
        rest = (bands, pad_tiles - n_tiles, 2 * q_count, LANES)
        tiles[:, n_tiles:] = jnp.zeros(rest, jnp.float32)

    def sum_band(band, carry):
        at = pl.ds(pl.multiple_of(band * wide, LANES), wide)
        total = jnp.dot(mix_ref[0], x_ref[0, :, at], preferred_element_type=jnp.float32)
        total += jnp.dot(mix_ref[1], x_ref[1, :, at], preferred_element_type=jnp.float32)
        for tile in range(n_tiles):
            tiles[band, tile] = total[:, tile * LANES : (tile + 1) * LANES]
        return carry

    lax.fori_loop(0, bands, sum_band, 0)

    def mode_copy(split, step):
        to = split * q_count + lax.rem(me + step, q_count)
        return to, pltpu.make_async_remote_copy(
            src_ref=staged.at[split, step],
            dst_ref=gathered.at[me],
            send_sem=mode_send.at[to],
            recv_sem=mode_recv.at[me],
            device_id={"re": to},
            device_id_type=MESH,
        )

    def mode_from(source):
        return pltpu.make_async_remote_copy(
            src_ref=staged.at[0, 0],
            dst_ref=gathered.at[source],
            send_sem=mode_send.at[source],
            recv_sem=mode_recv.at[source],
            device_id={"re": source},
            device_id_type=MESH,
        )

    nt = (((1,), (1,)), ((), ()))
    for q in range(q_count):
        q_at = lax.rem(me + q, q_count)
        ordered = []
        for part in range(2):
            first = lax.dot_general(
                order_ref[...], evec_ref[q_at, part], nt, preferred_element_type=jnp.float32
            ).astype(jnp.bfloat16)
            ordered.append(
                lax.dot_general(first, order_ref[...], nt, preferred_element_type=jnp.float32)
            )
        mode_mix = jnp.concatenate(
            [
                jnp.concatenate([ordered[0], -ordered[1]], axis=1),
                jnp.concatenate([ordered[1], ordered[0]], axis=1),
            ],
            axis=0,
        ).astype(jnp.bfloat16)
        rows = []
        for part in range(2):
            for group in range(groups):
                rows.append(
                    jnp.concatenate(
                        [
                            tiles[group * per + i, :, part * q_count + q, :].astype(jnp.bfloat16)
                            for i in range(per)
                        ],
                        axis=1,
                    )
                )
        swapped = jnp.dot(
            jnp.concatenate(rows, axis=0), swap_ref[...], preferred_element_type=jnp.float32
        ).astype(jnp.bfloat16)
        stacked = []
        for part in range(2):
            for i in range(per):
                stacked.append(
                    jnp.concatenate(
                        [
                            swapped[
                                (part * groups + group) * pad_tiles : (part * groups + group + 1)
                                * pad_tiles,
                                i * LANES : (i + 1) * LANES,
                            ]
                            for group in range(groups)
                        ],
                        axis=1,
                    )
                )
        moded = jnp.dot(
            mode_mix, jnp.concatenate(stacked, axis=0), preferred_element_type=jnp.float32
        ).astype(jnp.bfloat16)
        rows = []
        for part in range(2):
            for group in range(groups):
                rows.append(
                    jnp.concatenate(
                        [
                            moded[
                                (part * per + i) * pad_tiles : (part * per + i + 1) * pad_tiles,
                                group * LANES : (group + 1) * LANES,
                            ]
                            for i in range(per)
                        ],
                        axis=1,
                    )
                )
        back = jnp.dot(
            jnp.concatenate(rows, axis=0), swap_ref[...], preferred_element_type=jnp.float32
        )
        for part in range(2):
            for group in range(groups):
                for i in range(per):
                    turned[part * bands + group * per + i] = back[
                        (part * groups + group) * pad_tiles : (part * groups + group + 1)
                        * pad_tiles,
                        i * LANES : (i + 1) * LANES,
                    ]
        for tile in range(pad_tiles):
            place = tile % out_tiles
            staged[tile // out_tiles, q, :, place * LANES : (place + 1) * LANES] = turned[
                :, tile, :
            ].astype(jnp.bfloat16)

        def send_modes(split, carry):
            to, copy = mode_copy(split, q)

            @pl.when(to != me)
            def _():
                copy.start()

            return carry

        lax.fori_loop(0, splits, send_modes, 0)
    gathered[me] = staged[my_split, 0]

    def arrivals(i, carry):
        source = lax.rem(me + i, node_count)
        pack_from(source).wait_recv()
        mode_from(source).wait_recv()
        return carry

    lax.fori_loop(1, node_count, arrivals, 0)

    row = lax.broadcasted_iota(jnp.int32, (LANES, LANES), 0) // bands
    col = lax.broadcasted_iota(jnp.int32, (LANES, LANES), 1) // bands
    same = row == col
    nodes = batch // local_k
    place = pl.ds(pl.multiple_of(my_split * lanes, LANES), lanes)

    def power_copy(to):
        return pltpu.make_async_remote_copy(
            src_ref=power.at[pl.ds(to * local_k, local_k)],
            dst_ref=out_ref.at[:, my_q, :, place],
            send_sem=power_send.at[to],
            recv_sem=power_recv.at[me],
            device_id={"re": to},
            device_id_type=MESH,
        )

    def power_from(source):
        at = pl.ds(pl.multiple_of(source // q_count * lanes, LANES), lanes)
        return pltpu.make_async_remote_copy(
            src_ref=power.at[pl.ds(0, local_k)],
            dst_ref=out_ref.at[:, lax.rem(source, q_count), :, at],
            send_sem=power_send.at[source],
            recv_sem=power_recv.at[source],
            device_id={"re": source},
            device_id_type=MESH,
        )

    own_copy = pltpu.make_async_copy(
        power.at[pl.ds(me * local_k, local_k)], out_ref.at[:, my_q, :, place], own_sem
    )

    def rotate(i, carry):
        node = lax.rem(me // nodes + i + 1, node_count // nodes) * nodes
        base = node * local_k
        pack = jnp.concatenate(
            [packs[node + k // local_k, k % local_k] for k in range(batch)], axis=0
        )
        spread = jnp.dot(pack, widen_ref[...], preferred_element_type=jnp.float32)
        spread = [
            [spread[k * bands : (k + 1) * bands, t * LANES : (t + 1) * LANES] for t in range(5)]
            for k in range(batch)
        ]
        coeffs = []
        for k in range(batch):
            one = jnp.concatenate([spread[k][0], spread[k][1]], axis=0)
            two = jnp.concatenate([spread[k][2], spread[k][0]], axis=0)
            parts = []
            for tile in range(depth // LANES):
                lane = slice(tile * LANES, (tile + 1) * LANES)
                value = cos_ref[base + k, :, lane] * one + sin_ref[base + k, :, lane] * two
                parts.append(value.astype(jnp.bfloat16))
            coeffs.append(jnp.concatenate(parts, axis=1))
        half = jnp.dot(
            jnp.concatenate(coeffs, axis=0),
            gathered[...].reshape(depth, lanes),
            preferred_element_type=jnp.float32,
        ).astype(jnp.bfloat16)
        for k in range(batch):
            real = jnp.where(same, jnp.concatenate([spread[k][3]] * per, axis=0), 0.0)
            imag = jnp.where(same, jnp.concatenate([spread[k][4]] * per, axis=0), 0.0)
            both = jnp.concatenate(
                [
                    jnp.concatenate([real, -imag], axis=1),
                    jnp.concatenate([imag, real], axis=1),
                ],
                axis=0,
            ).astype(jnp.bfloat16)
            rows = []
            top = 2 * bands * k
            for tile in range(out_tiles):
                lane = slice(tile * LANES, (tile + 1) * LANES)
                rows.append(
                    jnp.concatenate(
                        [half[top : top + bands, lane], half[top + bands : top + 2 * bands, lane]],
                        axis=1,
                    )
                )
            final = jnp.dot(jnp.concatenate(rows, axis=0), both, preferred_element_type=jnp.float32)
            square = final[:, :LANES] * final[:, :LANES] + final[:, LANES:] * final[:, LANES:]
            square = square.astype(jnp.bfloat16)
            for tile in range(out_tiles):
                power[base + k, :, tile * LANES : (tile + 1) * LANES] = square[
                    tile * bands : (tile + 1) * bands
                ]
        for n in range(nodes):
            to = node + n

            @pl.when(to != me)
            def _():
                power_copy(to).start()

            @pl.when(to == me)
            def _():
                own_copy.start()

        return carry

    lax.fori_loop(0, node_count // nodes, rotate, 0)

    def finish(i, carry):
        other = lax.rem(me + i, node_count)
        pack_copy(other).wait_send()
        mode_from(other).wait_send()
        power_copy(other).wait_send()
        power_from(other).wait_recv()
        return carry

    lax.fori_loop(1, node_count, finish, 0)
    own_copy.wait()


def hand_over(node_count, value_ref, out_ref, came, send_sem, recv_sem):
    me = lax.axis_index("re")
    barrier = pltpu.get_barrier_semaphore()

    def greet(i, carry):
        other = lax.rem(me + i, node_count)
        pl.semaphore_signal(barrier, inc=1, device_id={"re": other}, device_id_type=MESH)
        return carry

    lax.fori_loop(1, node_count, greet, 0)
    pl.semaphore_wait(barrier, node_count - 1)

    def copy(to, slot):
        return pltpu.make_async_remote_copy(
            src_ref=value_ref.at[to],
            dst_ref=came.at[slot],
            send_sem=send_sem.at[to],
            recv_sem=recv_sem.at[slot],
            device_id={"re": to},
            device_id_type=MESH,
        )

    def send(i, carry):
        copy(lax.rem(me + i, node_count), me).start()
        return carry

    lax.fori_loop(1, node_count, send, 0)
    came[me] = value_ref[me]

    def finish(i, carry):
        other = lax.rem(me + i, node_count)
        copy(other, other).wait()
        return carry

    lax.fori_loop(1, node_count, finish, 0)
    out_ref[...] = jnp.sum(came[...], axis=0)


def rate_block(coupling_block, state_ids, eps_k, eps_kq, omega, temps):
    q_count = omega.shape[0]
    band_count = eps_k.shape[1]
    k_index = state_ids // (q_count * band_count)
    q_index = state_ids // band_count % q_count
    n_index = state_ids % band_count
    energy_n = eps_k[k_index, n_index]
    energy_m = eps_kq[k_index, q_index]
    phonon_freq = omega[q_index]
    strength = coupling_block.astype(jnp.float32)
    energy_gap = energy_n[:, None, None] - energy_m[:, None, :]
    peak_scale = broadening / jnp.pi
    lorentz_abs = peak_scale / ((energy_gap + phonon_freq[:, :, None]) ** 2 + broadening**2)
    lorentz_emit = peak_scale / ((energy_gap - phonon_freq[:, :, None]) ** 2 + broadening**2)
    along_mode = jnp.sum(strength * (lorentz_abs + lorentz_emit), axis=2)
    along_band = jnp.sum(strength * (lorentz_abs - lorentz_emit), axis=1)
    base_term = jnp.sum(strength * lorentz_emit, axis=(1, 2))
    bose_occ = 1.0 / jnp.expm1(phonon_freq[None, :, :] / temps[:, None, None])
    fermi_occ = jax.nn.sigmoid(-energy_m[None, :, :] / temps[:, None, None])
    rate_sum = (
        jnp.sum(bose_occ * along_mode[None], axis=2)
        + base_term[None]
        + jnp.sum(fermi_occ * along_band[None], axis=2)
    )
    return rate_sum / (strength.shape[1] * strength.shape[2])


def local(
    epmat,
    re_coords,
    rp_coords,
    q_coords,
    u_k,
    u_kq,
    evec,
    omega,
    eps_k,
    eps_kq,
    temps,
    owner_states,
):
    node_count = lax.axis_size("re")
    self_index = lax.axis_index("re")
    q_count = q_coords.shape[0]
    local_k = u_k.shape[0]
    count_k = local_k * node_count
    bands = u_k.shape[2]
    modes = evec.shape[2]
    wide = modes * bands
    per = LANES // bands
    n_tiles = wide // LANES
    splits = node_count // q_count
    pad_tiles = max(-(-n_tiles // 8) * 8, splits)
    lanes = pad_tiles // splits * LANES
    bf16 = jnp.bfloat16

    own_q = q_coords[(jnp.arange(q_count) + self_index) % q_count]
    cos_q, sin_q = phase_pair(own_q, rp_coords)
    mix = jnp.stack(
        [jnp.concatenate([cos_q, sin_q], axis=0), jnp.concatenate([-sin_q, cos_q], axis=0)], axis=0
    )
    cos_k, sin_k = phase_pair(fine_points(count_k), re_coords)
    cos_row = jnp.repeat(cos_k.astype(jnp.float32), 2 * bands, axis=1)[:, None, :]
    sin_row = jnp.repeat(sin_k.astype(jnp.float32), 2 * bands, axis=1)[:, None, :]
    depth = node_count * 2 * bands

    turned_k = u_k.transpose(0, 1, 3, 2)
    packs = jnp.stack(
        [
            jnp.concatenate([turned_k[:, 0], turned_k[:, 1], u_kq[:, q, 0], u_kq[:, q, 1]], axis=2)
            for q in range(q_count)
        ],
        axis=0,
    )

    batch = 2 * local_k
    dma = pltpu.SemaphoreType.DMA
    vmem = pl.BlockSpec(memory_space=pltpu.VMEM)
    power = pl.pallas_call(
        functools.partial(exchange, node_count, local_k, batch),
        in_specs=[vmem] * 9,
        out_specs=pl.BlockSpec(memory_space=pl.ANY),
        out_shape=jax.ShapeDtypeStruct((local_k, q_count, bands, splits * lanes), bf16),
        scratch_shapes=[
            pltpu.VMEM((bands, pad_tiles, 2 * q_count, LANES), jnp.float32),
            pltpu.VMEM((2 * bands, pad_tiles, LANES), jnp.float32),
            pltpu.VMEM((splits, q_count, 2 * bands, lanes), bf16),
            pltpu.VMEM((node_count, 2 * bands, lanes), bf16),
            pltpu.VMEM((node_count, local_k, bands, LANES), bf16),
            pltpu.VMEM((count_k, bands, lanes), bf16),
        ]
        + [dma((node_count,))] * 6
        + [dma],
        compiler_params=pltpu.CompilerParams(
            vmem_limit_bytes=56 * 2**20, collective_id=0, has_side_effects=True
        ),
        name="exchange",
    )(
        epmat[:, 0],
        mix,
        evec,
        packs,
        cos_row,
        sin_row,
        swap_matrix(bands),
        mode_order(modes, per, pad_tiles),
        widen_matrix(bands),
    )
    coupling = power[..., :wide]

    state_rows = coupling.reshape(-1, wide)
    state_total = state_rows.shape[0]
    capacity = owner_states.shape[1]
    run_count = capacity // SLOT
    runs = owner_states.reshape(node_count, run_count, SLOT)
    holds = runs[:, :, 0] // state_total == self_index
    picked = jnp.sum(jnp.where(holds[:, :, None], runs - self_index * state_total, 0), axis=1)
    picked = picked.reshape(-1)
    strength = state_rows[picked].reshape(-1, modes, bands)
    here = rate_block(
        strength, picked + self_index * state_total, eps_k, eps_kq, omega, temps
    )
    here = here.T.reshape(node_count, 1, SLOT, temps.shape[0])
    placed = jnp.where(holds[:, :, None, None], here, 0.0)
    placed = placed.reshape(node_count, capacity * temps.shape[0])
    width = -(-placed.shape[1] // (8 * LANES)) * 8 * LANES
    placed = jnp.pad(placed, ((0, 0), (0, width - placed.shape[1])))
    placed = placed.reshape(node_count, width // LANES, LANES)
    rates = pl.pallas_call(
        functools.partial(hand_over, node_count),
        in_specs=[vmem],
        out_specs=vmem,
        out_shape=jax.ShapeDtypeStruct(placed.shape[1:], jnp.float32),
        scratch_shapes=[pltpu.VMEM(placed.shape, jnp.float32)] + [dma((node_count,))] * 2,
        compiler_params=pltpu.CompilerParams(collective_id=1, has_side_effects=True),
        name="hand_over",
    )(placed)
    rates = rates.reshape(-1)[: capacity * temps.shape[0]]
    rates = rates.reshape(capacity, temps.shape[0]).T
    return (coupling, rates)


def solution(mesh):
    in_specs = (
        P(None, "re", None, None),
        P(),
        P(),
        P("grp", None),
        P("re", None, None, None),
        P("re", "grp", None, None, None),
        P("grp", None, None, None),
        P("grp", None),
        P(),
        P(None, "grp", None),
        P(),
        P("grp", None),
    )
    out_specs = (P("re", "grp", None, None), P("grp", "re"))
    return jax.shard_map(local, mesh=mesh, in_specs=in_specs, out_specs=out_specs, check_vma=False)
```

```python
import functools

import jax
import jax.numpy as jnp
import numpy as np
from jax import lax
from jax.experimental import pallas as pl
from jax.experimental.pallas import tpu as pltpu
from jax.sharding import PartitionSpec as P

GRID = 16
SLOT = 2
LANES = 128


broadening = 0.02


def phase_pair(left_vecs, right_vecs):
    dot_mod = jnp.sum(left_vecs[:, None, :] * right_vecs[None, :, :], axis=2) % GRID
    angles = 2.0 * jnp.pi / GRID * dot_mod.astype(jnp.float32)
    return (jnp.cos(angles).astype(jnp.bfloat16), jnp.sin(angles).astype(jnp.bfloat16))


def fine_points(point_count):
    point_index = jnp.arange(point_count, dtype=jnp.int32)
    return jnp.stack(
        [point_index % GRID, point_index // GRID % GRID, point_index // (GRID * GRID)], axis=1
    )


def pair_rows(first_part, second_part, stack_axis):
    upper = jnp.stack([first_part, second_part], axis=stack_axis)
    lower = jnp.stack([-second_part, first_part], axis=stack_axis)
    return jnp.stack([upper, lower], axis=stack_axis)


MESH = pl.DeviceIdType.MESH


def swap_matrix(bands):
    per = LANES // bands
    row = np.arange(per * LANES)
    image = (row // bands % per) * LANES + (row // LANES) * bands + row % bands
    return jnp.asarray(np.eye(per * LANES)[image], jnp.bfloat16)


def mode_order(modes, per, pad_tiles):
    row = np.arange(per * pad_tiles)
    source = (row % pad_tiles) * per + row // pad_tiles
    return jnp.asarray(source[:, None] == np.arange(modes)[None, :], jnp.bfloat16)


def widen_matrix(bands):
    per = LANES // bands
    out = np.zeros((LANES, 5 * LANES))
    plans = [
        [(0, 1), (1, -1)] * (per // 2),
        [(1, 1), (0, 1)] * (per // 2),
        [(1, -1), (0, -1)] * (per // 2),
        [(2, 1)] * per,
        [(3, 1)] * per,
    ]
    for tile, plan in enumerate(plans):
        for place, (source, sign) in enumerate(plan):
            for band in range(bands):
                out[source * bands + band, tile * LANES + place * bands + band] = sign
    return jnp.asarray(out, jnp.bfloat16)


def exchange(
    node_count,
    local_k,
    batch,
    x_ref,
    mix_ref,
    evec_ref,
    packs_ref,
    cos_ref,
    sin_ref,
    swap_ref,
    order_ref,
    widen_ref,
    out_ref,
    tiles,
    turned,
    staged,
    gathered,
    packs,
    power,
    pack_send,
    pack_recv,
    mode_send,
    mode_recv,
    power_send,
    power_recv,
    own_sem,
):
    q_count = evec_ref.shape[0]
    bands = packs_ref.shape[2]
    per = LANES // bands
    wide = x_ref.shape[3] // bands
    n_tiles = wide // LANES
    pad_tiles = tiles.shape[1]
    groups = bands // per
    lanes = staged.shape[3]
    out_tiles = lanes // LANES
    splits = staged.shape[0]
    depth = node_count * 2 * bands
    parts = 2 if out_tiles % 2 == 0 else 1
    part_tiles = out_tiles // parts

    me = lax.axis_index("re")
    my_q = lax.rem(me, q_count)
    my_split = me // q_count

    def sized(split, part, act):
        start = split * out_tiles + part * part_tiles
        rest = n_tiles % part_tiles

        @pl.when(start + part_tiles <= n_tiles)
        def _():
            act(part_tiles * LANES)

        if rest:

            @pl.when(start == n_tiles - rest)
            def _():
                act(rest * LANES)

    barrier = pltpu.get_barrier_semaphore()

    def greet(i, carry):
        other = lax.rem(me + i, node_count)
        pl.semaphore_signal(barrier, inc=1, device_id={"re": other}, device_id_type=MESH)
        return carry

    lax.fori_loop(1, node_count, greet, 0)
    pl.semaphore_wait(barrier, node_count - 1)

    def pack_copy(to):
        return pltpu.make_async_remote_copy(
            src_ref=packs_ref.at[lax.rem(to, q_count)],
            dst_ref=packs.at[me],
            send_sem=pack_send.at[to],
            recv_sem=pack_recv.at[me],
            device_id={"re": to},
            device_id_type=MESH,
        )

    def pack_from(source):
        return pltpu.make_async_remote_copy(
            src_ref=packs_ref.at[0],
            dst_ref=packs.at[source],
            send_sem=pack_send.at[source],
            recv_sem=pack_recv.at[source],
            device_id={"re": source},
            device_id_type=MESH,
        )

    def send_pack(i, carry):
        pack_copy(lax.rem(me + i, node_count)).start()
        return carry

    lax.fori_loop(1, node_count, send_pack, 0)
    packs[me] = packs_ref[my_q]

    if pad_tiles > n_tiles:
        rest = (bands, pad_tiles - n_tiles, 2 * q_count, LANES)
        tiles[:, n_tiles:] = jnp.zeros(rest, jnp.float32)

    def sum_band(band, carry):
        at = pl.ds(pl.multiple_of(band * wide, LANES), wide)
        total = jnp.dot(mix_ref[0], x_ref[0, 0, :, at], preferred_element_type=jnp.float32)
        total += jnp.dot(mix_ref[1], x_ref[1, 0, :, at], preferred_element_type=jnp.float32)
        for tile in range(n_tiles):
            tiles[band, tile] = total[:, tile * LANES : (tile + 1) * LANES]
        return carry

    lax.fori_loop(0, bands, sum_band, 0)

    def mode_copy(to, step, part, width):
        lane = pl.ds(part * part_tiles * LANES, width)
        return pltpu.make_async_remote_copy(
            src_ref=staged.at[to // q_count, step, :, lane],
            dst_ref=gathered.at[me, :, lane],
            send_sem=mode_send.at[part, to],
            recv_sem=mode_recv.at[part, me],
            device_id={"re": to},
            device_id_type=MESH,
        )

    def mode_from(source, part, width):
        lane = pl.ds(part * part_tiles * LANES, width)
        return pltpu.make_async_remote_copy(
            src_ref=staged.at[0, 0, :, lane],
            dst_ref=gathered.at[source, :, lane],
            send_sem=mode_send.at[part, source],
            recv_sem=mode_recv.at[part, source],
            device_id={"re": source},
            device_id_type=MESH,
        )

    def send_modes(step, part):
        def body(i, carry):
            split = lax.rem(my_split + i, splits)
            to = split * q_count + lax.rem(me + step, q_count)

            @pl.when(to != me)
            def _():
                sized(split, part, lambda width: mode_copy(to, step, part, width).start())

            return carry

        lax.fori_loop(0, splits, body, 0)

    nt = (((1,), (1,)), ((), ()))
    for q in range(q_count):
        q_at = lax.rem(me + q, q_count)
        ordered = []
        for part in range(2):
            first = lax.dot_general(
                order_ref[...], evec_ref[q_at, part], nt, preferred_element_type=jnp.float32
            ).astype(jnp.bfloat16)
            ordered.append(
                lax.dot_general(first, order_ref[...], nt, preferred_element_type=jnp.float32)
            )
        mode_mix = jnp.concatenate(
            [
                jnp.concatenate([ordered[0], -ordered[1]], axis=1),
                jnp.concatenate([ordered[1], ordered[0]], axis=1),
            ],
            axis=0,
        ).astype(jnp.bfloat16)
        rows = []
        for part in range(2):
            for group in range(groups):
                rows.append(
                    jnp.concatenate(
                        [
                            tiles[group * per + i, :, part * q_count + q, :].astype(jnp.bfloat16)
                            for i in range(per)
                        ],
                        axis=1,
                    )
                )
        swapped = jnp.dot(
            jnp.concatenate(rows, axis=0), swap_ref[...], preferred_element_type=jnp.float32
        ).astype(jnp.bfloat16)
        stacked = []
        for part in range(2):
            for i in range(per):
                stacked.append(
                    jnp.concatenate(
                        [
                            swapped[
                                (part * groups + group) * pad_tiles : (part * groups + group + 1)
                                * pad_tiles,
                                i * LANES : (i + 1) * LANES,
                            ]
                            for group in range(groups)
                        ],
                        axis=1,
                    )
                )
        moded = jnp.dot(
            mode_mix, jnp.concatenate(stacked, axis=0), preferred_element_type=jnp.float32
        ).astype(jnp.bfloat16)
        rows = []
        for part in range(2):
            for group in range(groups):
                rows.append(
                    jnp.concatenate(
                        [
                            moded[
                                (part * per + i) * pad_tiles : (part * per + i + 1) * pad_tiles,
                                group * LANES : (group + 1) * LANES,
                            ]
                            for i in range(per)
                        ],
                        axis=1,
                    )
                )
        back = jnp.dot(
            jnp.concatenate(rows, axis=0), swap_ref[...], preferred_element_type=jnp.float32
        )
        for part in range(2):
            for group in range(groups):
                for i in range(per):
                    turned[part * bands + group * per + i] = back[
                        (part * groups + group) * pad_tiles : (part * groups + group + 1)
                        * pad_tiles,
                        i * LANES : (i + 1) * LANES,
                    ]
        for tile in range(pad_tiles):
            place = tile % out_tiles
            staged[tile // out_tiles, q, :, place * LANES : (place + 1) * LANES] = turned[
                :, tile, :
            ].astype(jnp.bfloat16)

        send_modes(q, 0)
    for part in range(1, parts):
        for q in range(q_count):
            send_modes(q, part)
    gathered[me] = staged[my_split, 0]

    def packs_in(i, carry):
        pack_from(lax.rem(me + i, node_count)).wait_recv()
        return carry

    lax.fori_loop(1, node_count, packs_in, 0)

    row = lax.broadcasted_iota(jnp.int32, (LANES, LANES), 0) // bands
    col = lax.broadcasted_iota(jnp.int32, (LANES, LANES), 1) // bands
    same = row == col
    nodes = batch // local_k

    def power_copy(to, part, width):
        at = pl.multiple_of(my_split * lanes + part * part_tiles * LANES, LANES)
        return pltpu.make_async_remote_copy(
            src_ref=power.at[
                pl.ds(to * local_k, local_k), :, pl.ds(part * part_tiles * LANES, width)
            ],
            dst_ref=out_ref.at[:, my_q, :, pl.ds(at, width)],
            send_sem=power_send.at[part, to],
            recv_sem=power_recv.at[part, me],
            device_id={"re": to},
            device_id_type=MESH,
        )

    def power_from(source, part, width):
        at = source // q_count * lanes + part * part_tiles * LANES
        at = pl.multiple_of(at, LANES)
        return pltpu.make_async_remote_copy(
            src_ref=power.at[pl.ds(0, local_k), :, pl.ds(part * part_tiles * LANES, width)],
            dst_ref=out_ref.at[:, lax.rem(source, q_count), :, pl.ds(at, width)],
            send_sem=power_send.at[part, source],
            recv_sem=power_recv.at[part, source],
            device_id={"re": source},
            device_id_type=MESH,
        )

    def own_copy(part, width):
        at = pl.multiple_of(my_split * lanes + part * part_tiles * LANES, LANES)
        return pltpu.make_async_copy(
            power.at[pl.ds(me * local_k, local_k), :, pl.ds(part * part_tiles * LANES, width)],
            out_ref.at[:, my_q, :, pl.ds(at, width)],
            own_sem.at[part],
        )

    def rotate(part, i, carry):
        low = part * part_tiles * LANES
        node = lax.rem(me // nodes + i + 1, node_count // nodes) * nodes
        base = node * local_k
        pack = jnp.concatenate(
            [packs[node + k // local_k, k % local_k] for k in range(batch)], axis=0
        )
        spread = jnp.dot(pack, widen_ref[...], preferred_element_type=jnp.float32)
        spread = [
            [spread[k * bands : (k + 1) * bands, t * LANES : (t + 1) * LANES] for t in range(5)]
            for k in range(batch)
        ]
        coeffs = []
        for k in range(batch):
            one = jnp.concatenate([spread[k][0], spread[k][1]], axis=0)
            two = jnp.concatenate([spread[k][2], spread[k][0]], axis=0)
            parts = []
            for tile in range(depth // LANES):
                lane = slice(tile * LANES, (tile + 1) * LANES)
                value = cos_ref[base + k, :, lane] * one + sin_ref[base + k, :, lane] * two
                parts.append(value.astype(jnp.bfloat16))
            coeffs.append(jnp.concatenate(parts, axis=1))
        half = jnp.dot(
            jnp.concatenate(coeffs, axis=0),
            gathered[:, :, low : low + part_tiles * LANES].reshape(depth, part_tiles * LANES),
            preferred_element_type=jnp.float32,
        ).astype(jnp.bfloat16)
        for k in range(batch):
            real = jnp.where(same, jnp.concatenate([spread[k][3]] * per, axis=0), 0.0)
            imag = jnp.where(same, jnp.concatenate([spread[k][4]] * per, axis=0), 0.0)
            both = jnp.concatenate(
                [
                    jnp.concatenate([real, -imag], axis=1),
                    jnp.concatenate([imag, real], axis=1),
                ],
                axis=0,
            ).astype(jnp.bfloat16)
            rows = []
            top = 2 * bands * k
            for tile in range(part_tiles):
                lane = slice(tile * LANES, (tile + 1) * LANES)
                rows.append(
                    jnp.concatenate(
                        [half[top : top + bands, lane], half[top + bands : top + 2 * bands, lane]],
                        axis=1,
                    )
                )
            final = jnp.dot(jnp.concatenate(rows, axis=0), both, preferred_element_type=jnp.float32)
            square = final[:, :LANES] * final[:, :LANES] + final[:, LANES:] * final[:, LANES:]
            square = square.astype(jnp.bfloat16)
            for tile in range(part_tiles):
                lane = slice(low + tile * LANES, low + (tile + 1) * LANES)
                power[base + k, :, lane] = square[tile * bands : (tile + 1) * bands]
        for n in range(nodes):
            to = node + n

            @pl.when(to != me)
            def _():
                sized(my_split, part, lambda width: power_copy(to, part, width).start())

            @pl.when(to == me)
            def _():
                sized(my_split, part, lambda width: own_copy(part, width).start())

        return carry

    for part in range(parts):

        def modes_in(i, carry):
            source = lax.rem(me + i, node_count)
            sized(my_split, part, lambda width: mode_from(source, part, width).wait_recv())
            return carry

        lax.fori_loop(1, node_count, modes_in, 0)
        lax.fori_loop(0, node_count // nodes, functools.partial(rotate, part), 0)

    def finish(i, carry):
        other = lax.rem(me + i, node_count)
        split = other // q_count
        pack_copy(other).wait_send()
        for part in range(parts):
            sized(split, part, lambda width: mode_from(other, part, width).wait_send())
            sized(my_split, part, lambda width: power_copy(other, part, width).wait_send())
            sized(split, part, lambda width: power_from(other, part, width).wait_recv())
        return carry

    lax.fori_loop(1, node_count, finish, 0)
    for part in range(parts):
        sized(my_split, part, lambda width: own_copy(part, width).wait())


def hand_over(node_count, value_ref, out_ref, came, send_sem, recv_sem):
    me = lax.axis_index("re")
    barrier = pltpu.get_barrier_semaphore()

    def greet(i, carry):
        other = lax.rem(me + i, node_count)
        pl.semaphore_signal(barrier, inc=1, device_id={"re": other}, device_id_type=MESH)
        return carry

    lax.fori_loop(1, node_count, greet, 0)
    pl.semaphore_wait(barrier, node_count - 1)

    def copy(to, slot):
        return pltpu.make_async_remote_copy(
            src_ref=value_ref.at[to],
            dst_ref=came.at[slot],
            send_sem=send_sem.at[to],
            recv_sem=recv_sem.at[slot],
            device_id={"re": to},
            device_id_type=MESH,
        )

    def send(i, carry):
        copy(lax.rem(me + i, node_count), me).start()
        return carry

    lax.fori_loop(1, node_count, send, 0)
    came[me] = value_ref[me]

    def finish(i, carry):
        other = lax.rem(me + i, node_count)
        copy(other, other).wait()
        return carry

    lax.fori_loop(1, node_count, finish, 0)
    out_ref[...] = jnp.sum(came[...], axis=0)


def rate_block(coupling_block, state_ids, eps_k, eps_kq, omega, temps):
    q_count = omega.shape[0]
    band_count = eps_k.shape[1]
    k_index = state_ids // (q_count * band_count)
    q_index = state_ids // band_count % q_count
    n_index = state_ids % band_count
    energy_n = eps_k[k_index, n_index]
    energy_m = eps_kq[k_index, q_index]
    phonon_freq = omega[q_index]
    strength = coupling_block.astype(jnp.float32)
    energy_gap = energy_n[:, None, None] - energy_m[:, None, :]
    peak_scale = broadening / jnp.pi
    lorentz_abs = peak_scale / ((energy_gap + phonon_freq[:, :, None]) ** 2 + broadening**2)
    lorentz_emit = peak_scale / ((energy_gap - phonon_freq[:, :, None]) ** 2 + broadening**2)
    along_mode = jnp.sum(strength * (lorentz_abs + lorentz_emit), axis=2)
    along_band = jnp.sum(strength * (lorentz_abs - lorentz_emit), axis=1)
    base_term = jnp.sum(strength * lorentz_emit, axis=(1, 2))
    bose_occ = 1.0 / jnp.expm1(phonon_freq[None, :, :] / temps[:, None, None])
    fermi_occ = jax.nn.sigmoid(-energy_m[None, :, :] / temps[:, None, None])
    rate_sum = (
        jnp.sum(bose_occ * along_mode[None], axis=2)
        + base_term[None]
        + jnp.sum(fermi_occ * along_band[None], axis=2)
    )
    return rate_sum / (strength.shape[1] * strength.shape[2])


def local(
    epmat,
    re_coords,
    rp_coords,
    q_coords,
    u_k,
    u_kq,
    evec,
    omega,
    eps_k,
    eps_kq,
    temps,
    owner_states,
):
    node_count = lax.axis_size("re")
    self_index = lax.axis_index("re")
    q_count = q_coords.shape[0]
    local_k = u_k.shape[0]
    count_k = local_k * node_count
    bands = u_k.shape[2]
    modes = evec.shape[2]
    wide = modes * bands
    per = LANES // bands
    n_tiles = wide // LANES
    splits = node_count // q_count
    pad_tiles = max(-(-n_tiles // 8) * 8, splits)
    lanes = pad_tiles // splits * LANES
    bf16 = jnp.bfloat16

    own_q = q_coords[(jnp.arange(q_count) + self_index) % q_count]
    cos_q, sin_q = phase_pair(own_q, rp_coords)
    mix = jnp.stack(
        [jnp.concatenate([cos_q, sin_q], axis=0), jnp.concatenate([-sin_q, cos_q], axis=0)], axis=0
    )
    cos_k, sin_k = phase_pair(fine_points(count_k), re_coords)
    cos_row = jnp.repeat(cos_k.astype(jnp.float32), 2 * bands, axis=1)[:, None, :]
    sin_row = jnp.repeat(sin_k.astype(jnp.float32), 2 * bands, axis=1)[:, None, :]
    depth = node_count * 2 * bands

    turned_k = u_k.transpose(0, 1, 3, 2)
    packs = jnp.stack(
        [
            jnp.concatenate([turned_k[:, 0], turned_k[:, 1], u_kq[:, q, 0], u_kq[:, q, 1]], axis=2)
            for q in range(q_count)
        ],
        axis=0,
    )

    batch = 2 * local_k
    dma = pltpu.SemaphoreType.DMA
    vmem = pl.BlockSpec(memory_space=pltpu.VMEM)
    coupling = pl.pallas_call(
        functools.partial(exchange, node_count, local_k, batch),
        in_specs=[vmem] * 9,
        out_specs=pl.BlockSpec(memory_space=pl.ANY),
        out_shape=jax.ShapeDtypeStruct((local_k, q_count, bands, wide), bf16),
        scratch_shapes=[
            pltpu.VMEM((bands, pad_tiles, 2 * q_count, LANES), jnp.float32),
            pltpu.VMEM((2 * bands, pad_tiles, LANES), jnp.float32),
            pltpu.VMEM((splits, q_count, 2 * bands, lanes), bf16),
            pltpu.VMEM((node_count, 2 * bands, lanes), bf16),
            pltpu.VMEM((node_count, local_k, bands, LANES), bf16),
            pltpu.VMEM((count_k, bands, lanes), bf16),
        ]
        + [dma((node_count,))] * 2
        + [dma((2, node_count))] * 4
        + [dma((2,))],
        compiler_params=pltpu.CompilerParams(
            vmem_limit_bytes=56 * 2**20, collective_id=0, has_side_effects=True
        ),
        name="exchange",
    )(
        epmat,
        mix,
        evec,
        packs,
        cos_row,
        sin_row,
        swap_matrix(bands),
        mode_order(modes, per, pad_tiles),
        widen_matrix(bands),
    )

    state_rows = coupling.reshape(-1, wide)
    state_total = state_rows.shape[0]
    capacity = owner_states.shape[1]
    run_count = capacity // SLOT
    runs = owner_states.reshape(node_count, run_count, SLOT)
    holds = runs[:, :, 0] // state_total == self_index
    picked = jnp.sum(jnp.where(holds[:, :, None], runs - self_index * state_total, 0), axis=1)
    picked = picked.reshape(-1)
    strength = state_rows[picked].reshape(-1, modes, bands)
    here = rate_block(
        strength, picked + self_index * state_total, eps_k, eps_kq, omega, temps
    )
    here = here.T.reshape(node_count, 1, SLOT, temps.shape[0])
    placed = jnp.where(holds[:, :, None, None], here, 0.0)
    placed = placed.reshape(node_count, capacity * temps.shape[0])
    width = -(-placed.shape[1] // (8 * LANES)) * 8 * LANES
    placed = jnp.pad(placed, ((0, 0), (0, width - placed.shape[1])))
    placed = placed.reshape(node_count, width // LANES, LANES)
    rates = pl.pallas_call(
        functools.partial(hand_over, node_count),
        in_specs=[vmem],
        out_specs=vmem,
        out_shape=jax.ShapeDtypeStruct(placed.shape[1:], jnp.float32),
        scratch_shapes=[pltpu.VMEM(placed.shape, jnp.float32)] + [dma((node_count,))] * 2,
        compiler_params=pltpu.CompilerParams(collective_id=1, has_side_effects=True),
        name="hand_over",
    )(placed)
    rates = rates.reshape(-1)[: capacity * temps.shape[0]]
    rates = rates.reshape(capacity, temps.shape[0]).T
    return (coupling, rates)


def solution(mesh):
    in_specs = (
        P(None, "re", None, None),
        P(),
        P(),
        P("grp", None),
        P("re", None, None, None),
        P("re", "grp", None, None, None),
        P("grp", None, None, None),
        P("grp", None),
        P(),
        P(None, "grp", None),
        P(),
        P("grp", None),
    )
    out_specs = (P("re", "grp", None, None), P("grp", "re"))
    return jax.shard_map(local, mesh=mesh, in_specs=in_specs, out_specs=out_specs, check_vma=False)
```

```python
import functools

import jax
import jax.numpy as jnp
import numpy as np
from jax import lax
from jax.experimental import pallas as pl
from jax.experimental.pallas import tpu as pltpu
from jax.sharding import PartitionSpec as P

GRID = 16
SLOT = 2
LANES = 128


broadening = 0.02


def phase_pair(left_vecs, right_vecs):
    dot_mod = jnp.sum(left_vecs[:, None, :] * right_vecs[None, :, :], axis=2) % GRID
    angles = 2.0 * jnp.pi / GRID * dot_mod.astype(jnp.float32)
    return (jnp.cos(angles).astype(jnp.bfloat16), jnp.sin(angles).astype(jnp.bfloat16))


def fine_points(point_count):
    point_index = jnp.arange(point_count, dtype=jnp.int32)
    return jnp.stack(
        [point_index % GRID, point_index // GRID % GRID, point_index // (GRID * GRID)], axis=1
    )


def pair_rows(first_part, second_part, stack_axis):
    upper = jnp.stack([first_part, second_part], axis=stack_axis)
    lower = jnp.stack([-second_part, first_part], axis=stack_axis)
    return jnp.stack([upper, lower], axis=stack_axis)


MESH = pl.DeviceIdType.MESH


def swap_matrix(bands):
    per = LANES // bands
    row = np.arange(per * LANES)
    image = (row // bands % per) * LANES + (row // LANES) * bands + row % bands
    return jnp.asarray(np.eye(per * LANES)[image], jnp.bfloat16)


def mode_order(modes, per, pad_tiles):
    row = np.arange(per * pad_tiles)
    source = (row % pad_tiles) * per + row // pad_tiles
    return jnp.asarray(source[:, None] == np.arange(modes)[None, :], jnp.bfloat16)


def widen_matrix(bands):
    per = LANES // bands
    out = np.zeros((LANES, 5 * LANES))
    plans = [
        [(0, 1), (1, -1)] * (per // 2),
        [(1, 1), (0, 1)] * (per // 2),
        [(1, -1), (0, -1)] * (per // 2),
        [(2, 1)] * per,
        [(3, 1)] * per,
    ]
    for tile, plan in enumerate(plans):
        for place, (source, sign) in enumerate(plan):
            for band in range(bands):
                out[source * bands + band, tile * LANES + place * bands + band] = sign
    return jnp.asarray(out, jnp.bfloat16)


def exchange(
    node_count,
    local_k,
    batch,
    x_ref,
    mix_ref,
    evec_ref,
    packs_ref,
    wave_ref,
    swap_ref,
    order_ref,
    widen_ref,
    out_ref,
    tiles,
    turned,
    staged,
    gathered,
    packs,
    power,
    pack_send,
    pack_recv,
    mode_send,
    mode_recv,
    power_send,
    power_recv,
    own_sem,
):
    q_count = evec_ref.shape[0]
    bands = packs_ref.shape[2]
    per = LANES // bands
    wide = x_ref.shape[3] // bands
    n_tiles = wide // LANES
    pad_tiles = tiles.shape[1]
    groups = bands // per
    lanes = staged.shape[3]
    out_tiles = lanes // LANES
    splits = staged.shape[0]
    depth = node_count * 2 * bands
    parts = 2 if out_tiles % 2 == 0 else 1
    part_tiles = out_tiles // parts

    me = lax.axis_index("re")
    my_q = lax.rem(me, q_count)
    my_split = me // q_count

    def sized(split, part, act):
        start = split * out_tiles + part * part_tiles
        rest = n_tiles % part_tiles

        @pl.when(start + part_tiles <= n_tiles)
        def _():
            act(part_tiles * LANES)

        if rest:

            @pl.when(start == n_tiles - rest)
            def _():
                act(rest * LANES)

    barrier = pltpu.get_barrier_semaphore()

    def greet(i, carry):
        other = lax.rem(me + i, node_count)
        pl.semaphore_signal(barrier, inc=1, device_id={"re": other}, device_id_type=MESH)
        return carry

    lax.fori_loop(1, node_count, greet, 0)
    pl.semaphore_wait(barrier, node_count - 1)

    def pack_copy(to):
        return pltpu.make_async_remote_copy(
            src_ref=packs_ref.at[lax.rem(to, q_count)],
            dst_ref=packs.at[me],
            send_sem=pack_send.at[to],
            recv_sem=pack_recv.at[me],
            device_id={"re": to},
            device_id_type=MESH,
        )

    def pack_from(source):
        return pltpu.make_async_remote_copy(
            src_ref=packs_ref.at[0],
            dst_ref=packs.at[source],
            send_sem=pack_send.at[source],
            recv_sem=pack_recv.at[source],
            device_id={"re": source},
            device_id_type=MESH,
        )

    def send_pack(i, carry):
        pack_copy(lax.rem(me + i, node_count)).start()
        return carry

    lax.fori_loop(1, node_count, send_pack, 0)
    packs[me] = packs_ref[my_q]

    if pad_tiles > n_tiles:
        rest = (bands, pad_tiles - n_tiles, 2 * q_count, LANES)
        tiles[:, n_tiles:] = jnp.zeros(rest, jnp.float32)

    def sum_bands(group, carry):
        for i in range(per):
            band = group * per + i
            at = pl.ds(pl.multiple_of(band * wide, LANES), wide)
            total = jnp.dot(mix_ref[0], x_ref[0, 0, :, at], preferred_element_type=jnp.float32)
            total += jnp.dot(mix_ref[1], x_ref[1, 0, :, at], preferred_element_type=jnp.float32)
            for tile in range(n_tiles):
                tiles[band, tile] = total[:, tile * LANES : (tile + 1) * LANES]
        return carry

    lax.fori_loop(0, groups, sum_bands, 0)

    def mode_copy(to, step, part, width):
        lane = pl.ds(part * part_tiles * LANES, width)
        return pltpu.make_async_remote_copy(
            src_ref=staged.at[to // q_count, step, :, lane],
            dst_ref=gathered.at[me, :, lane],
            send_sem=mode_send.at[part, to],
            recv_sem=mode_recv.at[part, me],
            device_id={"re": to},
            device_id_type=MESH,
        )

    def mode_from(source, part, width):
        lane = pl.ds(part * part_tiles * LANES, width)
        return pltpu.make_async_remote_copy(
            src_ref=staged.at[0, 0, :, lane],
            dst_ref=gathered.at[source, :, lane],
            send_sem=mode_send.at[part, source],
            recv_sem=mode_recv.at[part, source],
            device_id={"re": source},
            device_id_type=MESH,
        )

    def send_modes(step, part):
        def body(i, carry):
            split = lax.rem(my_split + i, splits)
            to = split * q_count + lax.rem(me + step, q_count)

            @pl.when(to != me)
            def _():
                sized(split, part, lambda width: mode_copy(to, step, part, width).start())

            return carry

        lax.fori_loop(0, splits, body, 0)

    nt = (((1,), (1,)), ((), ()))
    for q in range(q_count):
        q_at = lax.rem(me + q, q_count)
        ordered = []
        for part in range(2):
            first = lax.dot_general(
                order_ref[...], evec_ref[q_at, part], nt, preferred_element_type=jnp.float32
            ).astype(jnp.bfloat16)
            ordered.append(
                lax.dot_general(first, order_ref[...], nt, preferred_element_type=jnp.float32)
            )
        mode_mix = jnp.concatenate(
            [
                jnp.concatenate([ordered[0], -ordered[1]], axis=1),
                jnp.concatenate([ordered[1], ordered[0]], axis=1),
            ],
            axis=0,
        ).astype(jnp.bfloat16)
        rows = []
        for part in range(2):
            for group in range(groups):
                rows.append(
                    jnp.concatenate(
                        [
                            tiles[group * per + i, :, part * q_count + q, :].astype(jnp.bfloat16)
                            for i in range(per)
                        ],
                        axis=1,
                    )
                )
        swapped = jnp.dot(
            jnp.concatenate(rows, axis=0), swap_ref[...], preferred_element_type=jnp.float32
        ).astype(jnp.bfloat16)
        stacked = []
        for part in range(2):
            for i in range(per):
                stacked.append(
                    jnp.concatenate(
                        [
                            swapped[
                                (part * groups + group) * pad_tiles : (part * groups + group + 1)
                                * pad_tiles,
                                i * LANES : (i + 1) * LANES,
                            ]
                            for group in range(groups)
                        ],
                        axis=1,
                    )
                )
        moded = jnp.dot(
            mode_mix, jnp.concatenate(stacked, axis=0), preferred_element_type=jnp.float32
        ).astype(jnp.bfloat16)
        rows = []
        for part in range(2):
            for group in range(groups):
                rows.append(
                    jnp.concatenate(
                        [
                            moded[
                                (part * per + i) * pad_tiles : (part * per + i + 1) * pad_tiles,
                                group * LANES : (group + 1) * LANES,
                            ]
                            for i in range(per)
                        ],
                        axis=1,
                    )
                )
        back = jnp.dot(
            jnp.concatenate(rows, axis=0), swap_ref[...], preferred_element_type=jnp.float32
        )
        for part in range(2):
            for group in range(groups):
                for i in range(per):
                    turned[part * bands + group * per + i] = back[
                        (part * groups + group) * pad_tiles : (part * groups + group + 1)
                        * pad_tiles,
                        i * LANES : (i + 1) * LANES,
                    ]
        for tile in range(pad_tiles):
            place = tile % out_tiles
            staged[tile // out_tiles, q, :, place * LANES : (place + 1) * LANES] = turned[
                :, tile, :
            ].astype(jnp.bfloat16)

        send_modes(q, 0)
    for part in range(1, parts):
        for q in range(q_count):
            send_modes(q, part)
    gathered[me] = staged[my_split, 0]

    def packs_in(i, carry):
        pack_from(lax.rem(me + i, node_count)).wait_recv()
        return carry

    lax.fori_loop(1, node_count, packs_in, 0)

    row = lax.broadcasted_iota(jnp.int32, (LANES, LANES), 0) // bands
    col = lax.broadcasted_iota(jnp.int32, (LANES, LANES), 1) // bands
    same = row == col
    nodes = batch // local_k

    def power_copy(to, part, width):
        at = pl.multiple_of(my_split * lanes + part * part_tiles * LANES, LANES)
        return pltpu.make_async_remote_copy(
            src_ref=power.at[
                pl.ds(to * local_k, local_k), :, pl.ds(part * part_tiles * LANES, width)
            ],
            dst_ref=out_ref.at[:, my_q, :, pl.ds(at, width)],
            send_sem=power_send.at[part, to],
            recv_sem=power_recv.at[part, me],
            device_id={"re": to},
            device_id_type=MESH,
        )

    def power_from(source, part, width):
        at = source // q_count * lanes + part * part_tiles * LANES
        at = pl.multiple_of(at, LANES)
        return pltpu.make_async_remote_copy(
            src_ref=power.at[pl.ds(0, local_k), :, pl.ds(part * part_tiles * LANES, width)],
            dst_ref=out_ref.at[:, lax.rem(source, q_count), :, pl.ds(at, width)],
            send_sem=power_send.at[part, source],
            recv_sem=power_recv.at[part, source],
            device_id={"re": source},
            device_id_type=MESH,
        )

    def own_copy(part, width):
        at = pl.multiple_of(my_split * lanes + part * part_tiles * LANES, LANES)
        return pltpu.make_async_copy(
            power.at[pl.ds(me * local_k, local_k), :, pl.ds(part * part_tiles * LANES, width)],
            out_ref.at[:, my_q, :, pl.ds(at, width)],
            own_sem.at[part],
        )

    def rotate(part, i, carry):
        low = part * part_tiles * LANES
        node = lax.rem(me // nodes + i + 1, node_count // nodes) * nodes
        base = node * local_k
        pack = jnp.concatenate(
            [packs[node + k // local_k, k % local_k] for k in range(batch)], axis=0
        )
        spread = jnp.dot(pack, widen_ref[...], preferred_element_type=jnp.float32)
        spread = [
            [spread[k * bands : (k + 1) * bands, t * LANES : (t + 1) * LANES] for t in range(5)]
            for k in range(batch)
        ]
        coeffs = []
        for k in range(batch):
            one = jnp.concatenate([spread[k][0], spread[k][1]], axis=0)
            two = jnp.concatenate([spread[k][2], spread[k][0]], axis=0)
            wave = wave_ref[base + k]
            parts = []
            for tile in range(depth // LANES):
                lane = slice(tile * LANES, (tile + 1) * LANES)
                value = wave[0:1, lane] * one + wave[1:2, lane] * two
                parts.append(value.astype(jnp.bfloat16))
            coeffs.append(jnp.concatenate(parts, axis=1))
        half = jnp.dot(
            jnp.concatenate(coeffs, axis=0),
            gathered[:, :, low : low + part_tiles * LANES].reshape(depth, part_tiles * LANES),
            preferred_element_type=jnp.float32,
        ).astype(jnp.bfloat16)
        for k in range(batch):
            real = jnp.where(same, jnp.concatenate([spread[k][3]] * per, axis=0), 0.0)
            imag = jnp.where(same, jnp.concatenate([spread[k][4]] * per, axis=0), 0.0)
            both = jnp.concatenate(
                [
                    jnp.concatenate([real, -imag], axis=1),
                    jnp.concatenate([imag, real], axis=1),
                ],
                axis=0,
            ).astype(jnp.bfloat16)
            rows = []
            top = 2 * bands * k
            for tile in range(part_tiles):
                lane = slice(tile * LANES, (tile + 1) * LANES)
                rows.append(
                    jnp.concatenate(
                        [half[top : top + bands, lane], half[top + bands : top + 2 * bands, lane]],
                        axis=1,
                    )
                )
            final = jnp.dot(jnp.concatenate(rows, axis=0), both, preferred_element_type=jnp.float32)
            square = final[:, :LANES] * final[:, :LANES] + final[:, LANES:] * final[:, LANES:]
            square = square.astype(jnp.bfloat16)
            for tile in range(part_tiles):
                lane = slice(low + tile * LANES, low + (tile + 1) * LANES)
                power[base + k, :, lane] = square[tile * bands : (tile + 1) * bands]
        for n in range(nodes):
            to = node + n

            @pl.when(to != me)
            def _():
                sized(my_split, part, lambda width: power_copy(to, part, width).start())

            @pl.when(to == me)
            def _():
                sized(my_split, part, lambda width: own_copy(part, width).start())

        return carry

    for part in range(parts):

        def modes_in(i, carry):
            source = lax.rem(me + i, node_count)
            sized(my_split, part, lambda width: mode_from(source, part, width).wait_recv())
            return carry

        lax.fori_loop(1, node_count, modes_in, 0)
        lax.fori_loop(0, node_count // nodes, functools.partial(rotate, part), 0)

    def finish(i, carry):
        other = lax.rem(me + i, node_count)
        split = other // q_count
        pack_copy(other).wait_send()
        for part in range(parts):
            sized(split, part, lambda width: mode_from(other, part, width).wait_send())
            sized(my_split, part, lambda width: power_copy(other, part, width).wait_send())
            sized(split, part, lambda width: power_from(other, part, width).wait_recv())
        return carry

    lax.fori_loop(1, node_count, finish, 0)
    for part in range(parts):
        sized(my_split, part, lambda width: own_copy(part, width).wait())


def hand_over(node_count, value_ref, out_ref, came, send_sem, recv_sem):
    me = lax.axis_index("re")
    barrier = pltpu.get_barrier_semaphore()

    def greet(i, carry):
        other = lax.rem(me + i, node_count)
        pl.semaphore_signal(barrier, inc=1, device_id={"re": other}, device_id_type=MESH)
        return carry

    lax.fori_loop(1, node_count, greet, 0)
    pl.semaphore_wait(barrier, node_count - 1)

    def copy(to, slot):
        return pltpu.make_async_remote_copy(
            src_ref=value_ref.at[to],
            dst_ref=came.at[slot],
            send_sem=send_sem.at[to],
            recv_sem=recv_sem.at[slot],
            device_id={"re": to},
            device_id_type=MESH,
        )

    def send(i, carry):
        copy(lax.rem(me + i, node_count), me).start()
        return carry

    lax.fori_loop(1, node_count, send, 0)
    came[me] = value_ref[me]

    def finish(i, carry):
        other = lax.rem(me + i, node_count)
        copy(other, other).wait()
        return carry

    lax.fori_loop(1, node_count, finish, 0)
    out_ref[...] = jnp.sum(came[...], axis=0)


def rate_block(coupling_block, state_ids, eps_k, eps_kq, omega, temps):
    q_count = omega.shape[0]
    band_count = eps_k.shape[1]
    k_index = state_ids // (q_count * band_count)
    q_index = state_ids // band_count % q_count
    n_index = state_ids % band_count
    energy_n = eps_k[k_index, n_index]
    energy_m = eps_kq[k_index, q_index]
    phonon_freq = omega[q_index]
    strength = coupling_block.astype(jnp.float32)
    energy_gap = energy_n[:, None, None] - energy_m[:, None, :]
    peak_scale = broadening / jnp.pi
    lorentz_abs = peak_scale / ((energy_gap + phonon_freq[:, :, None]) ** 2 + broadening**2)
    lorentz_emit = peak_scale / ((energy_gap - phonon_freq[:, :, None]) ** 2 + broadening**2)
    along_mode = jnp.sum(strength * (lorentz_abs + lorentz_emit), axis=2)
    along_band = jnp.sum(strength * (lorentz_abs - lorentz_emit), axis=1)
    base_term = jnp.sum(strength * lorentz_emit, axis=(1, 2))
    bose_occ = 1.0 / jnp.expm1(phonon_freq[None, :, :] / temps[:, None, None])
    fermi_occ = jax.nn.sigmoid(-energy_m[None, :, :] / temps[:, None, None])
    rate_sum = (
        jnp.sum(bose_occ * along_mode[None], axis=2)
        + base_term[None]
        + jnp.sum(fermi_occ * along_band[None], axis=2)
    )
    return rate_sum / (strength.shape[1] * strength.shape[2])


def local(
    epmat,
    re_coords,
    rp_coords,
    q_coords,
    u_k,
    u_kq,
    evec,
    omega,
    eps_k,
    eps_kq,
    temps,
    owner_states,
):
    node_count = lax.axis_size("re")
    self_index = lax.axis_index("re")
    q_count = q_coords.shape[0]
    local_k = u_k.shape[0]
    count_k = local_k * node_count
    bands = u_k.shape[2]
    modes = evec.shape[2]
    wide = modes * bands
    per = LANES // bands
    n_tiles = wide // LANES
    splits = node_count // q_count
    pad_tiles = max(-(-n_tiles // 8) * 8, splits)
    lanes = pad_tiles // splits * LANES
    bf16 = jnp.bfloat16

    twice = jnp.concatenate([q_coords, q_coords], axis=0)
    own_q = lax.dynamic_slice_in_dim(twice, self_index % q_count, q_count, 0)
    cos_q, sin_q = phase_pair(own_q, rp_coords)
    mix = jnp.stack(
        [jnp.concatenate([cos_q, sin_q], axis=0), jnp.concatenate([-sin_q, cos_q], axis=0)], axis=0
    )
    cos_k, sin_k = phase_pair(fine_points(count_k), re_coords)
    waves = jnp.stack([cos_k, sin_k], axis=1).astype(jnp.float32)
    waves = jnp.repeat(waves, 2 * bands, axis=2)
    depth = node_count * 2 * bands

    turned_k = u_k.transpose(0, 1, 3, 2)
    packs = jnp.stack(
        [
            jnp.concatenate([turned_k[:, 0], turned_k[:, 1], u_kq[:, q, 0], u_kq[:, q, 1]], axis=2)
            for q in range(q_count)
        ],
        axis=0,
    )

    batch = 2 * local_k
    dma = pltpu.SemaphoreType.DMA
    vmem = pl.BlockSpec(memory_space=pltpu.VMEM)
    coupling = pl.pallas_call(
        functools.partial(exchange, node_count, local_k, batch),
        in_specs=[vmem] * 8,
        out_specs=pl.BlockSpec(memory_space=pl.ANY),
        out_shape=jax.ShapeDtypeStruct((local_k, q_count, bands, wide), bf16),
        scratch_shapes=[
            pltpu.VMEM((bands, pad_tiles, 2 * q_count, LANES), jnp.float32),
            pltpu.VMEM((2 * bands, pad_tiles, LANES), jnp.float32),
            pltpu.VMEM((splits, q_count, 2 * bands, lanes), bf16),
            pltpu.VMEM((node_count, 2 * bands, lanes), bf16),
            pltpu.VMEM((node_count, local_k, bands, LANES), bf16),
            pltpu.VMEM((count_k, bands, lanes), bf16),
        ]
        + [dma((node_count,))] * 2
        + [dma((2, node_count))] * 4
        + [dma((2,))],
        compiler_params=pltpu.CompilerParams(
            vmem_limit_bytes=56 * 2**20, collective_id=0, has_side_effects=True
        ),
        name="exchange",
    )(
        epmat,
        mix,
        evec,
        packs,
        waves,
        swap_matrix(bands),
        mode_order(modes, per, pad_tiles),
        widen_matrix(bands),
    )

    state_rows = coupling.reshape(-1, wide)
    state_total = state_rows.shape[0]
    capacity = owner_states.shape[1]
    run_count = capacity // SLOT
    runs = owner_states.reshape(node_count, run_count, SLOT)
    holds = runs[:, :, 0] // state_total == self_index
    picked = jnp.sum(jnp.where(holds[:, :, None], runs - self_index * state_total, 0), axis=1)
    picked = picked.reshape(-1)
    strength = state_rows[picked].reshape(-1, modes, bands)
    here = rate_block(
        strength, picked + self_index * state_total, eps_k, eps_kq, omega, temps
    )
    here = here.T.reshape(node_count, 1, SLOT, temps.shape[0])
    placed = jnp.where(holds[:, :, None, None], here, 0.0)
    placed = placed.reshape(node_count, capacity * temps.shape[0])
    width = -(-placed.shape[1] // (8 * LANES)) * 8 * LANES
    placed = jnp.pad(placed, ((0, 0), (0, width - placed.shape[1])))
    placed = placed.reshape(node_count, width // LANES, LANES)
    rates = pl.pallas_call(
        functools.partial(hand_over, node_count),
        in_specs=[vmem],
        out_specs=vmem,
        out_shape=jax.ShapeDtypeStruct(placed.shape[1:], jnp.float32),
        scratch_shapes=[pltpu.VMEM(placed.shape, jnp.float32)] + [dma((node_count,))] * 2,
        compiler_params=pltpu.CompilerParams(collective_id=1, has_side_effects=True),
        name="hand_over",
    )(placed)
    rates = rates.reshape(-1)[: capacity * temps.shape[0]]
    rates = rates.reshape(capacity, temps.shape[0]).T
    return (coupling, rates)


def solution(mesh):
    in_specs = (
        P(None, "re", None, None),
        P(),
        P(),
        P("grp", None),
        P("re", None, None, None),
        P("re", "grp", None, None, None),
        P("grp", None, None, None),
        P("grp", None),
        P(),
        P(None, "grp", None),
        P(),
        P("grp", None),
    )
    out_specs = (P("re", "grp", None, None), P("grp", "re"))
    return jax.shard_map(local, mesh=mesh, in_specs=in_specs, out_specs=out_specs, check_vma=False)
```
